32 devices in a mesh: sec: 4 (over z), dom: 8 (over y, x, core).
Axes of the slice: x: 2, y: 2, z: 4, core: 2. Of those that a mesh axis runs over, the one named last changes fastest.
Arguments:
- rhs: float32 [256, 2048], P(('sec', 'dom')), may hold values from -6 to 6
- fine_blocks: float32 [256, 8, 4096], P(('sec', 'dom')), may hold values from -1 to 3
- fine_columns: int32 [256, 8], P(('sec', 'dom')), may hold values from 0 to 39, as said below
- send_lists: int32 [32, 4, 8], P(('sec', 'dom')), may hold values from -1 to 7, as said below
- smoother: bfloat16 [256, 4096], P(('sec', 'dom')), may hold values from -1 to 1
- prolong: bfloat16 [256, 384], P(('sec', 'dom')), may hold values from -4.1875 to 4.1875
- agg_map: int32 [256], P(('sec', 'dom')), may hold values from 0 to 1, as said below
- coarse_blocks: float32 [64, 8, 36], P(('sec', 'dom')), may hold values from -2 to 4
- coarse_columns: int32 [64, 8], P(('sec', 'dom')), may hold values from 0 to 63, as said below
- coarse_smoother: float32 [64, 36], P(('sec', 'dom')), may hold values from -1 to 1.5
Outputs:
- solution: float32 [256, 2048], P(('sec', 'dom'))
- coarse_solution: float32 [64, 192], P(('sec', 'dom'))
The draws below stay inside these ranges and needn't reach their ends.
Inputs may be any that keep to these rules, and one draw needn't show every extreme that they name: `fine_columns`: slot 0 of a row names the row itself; the other slots name own rows or halo rows of the extended array. `send_lists`: each entry is a block row of the sender or -1 for an empty slot; empty slots come last and every list has at least 4 filled slots. `agg_map`: every aggregate of a device holds at least one of its block rows. `coarse_columns`: slot 0 of a row names the row itself. Slots 1, 2, 3, 4 name an aggregate of device (s, d-1), (s, d+1), (s-1, d), (s+1, d) respectively, where (s, d) is the row's device, or the row itself where that device does not exist. The other slots may name any aggregate.
All inputs are finite; a program needn't handle non-finite values.
Results may differ from the reference program's by a relative error of at most 0.012.
Values sent between devices are 32-bit elements; how exact they have to be, the bound alone decides.
A program may use at most 128 MiB of HBM per device.

```python
import math
import jax
import jax.numpy as jnp
from jax import lax

B = 64
R = 32
BC = 6
K = 8
KC = 8
HS = 8
NBLK = 8
NPRE = 5
NPOST = 5
CITERS = 4
NAGG = 2
NFB = 256
NCOARSE = 64
N_SEC = 4
N_DOM = 8
DEVICES = 32


def dominant_blocks(key, rows, slots, width, scale):
    noise = jnp.clip(jax.random.normal(key, (rows, slots, width * width), jnp.float32), -6.0, 6.0)
    values = noise * (scale / math.sqrt(width))
    identity = jnp.eye(width, dtype=jnp.float32).reshape(width * width)
    first = (jnp.arange(slots) == 0).astype(jnp.float32)
    return values + 2.0 * first[None, :, None] * identity[None, None, :]


def near_inverse(key, rows, width, spread):
    noise = jnp.clip(jax.random.normal(key, (rows, width * width), jnp.float32), -6.0, 6.0)
    identity = jnp.eye(width, dtype=jnp.float32).reshape(width * width)
    return 0.45 * identity[None, :] + noise * (spread / math.sqrt(width))


def draw_fine_blocks(key, part):
    key = jax.random.fold_in(key, 11)
    return dominant_blocks(key, NFB, K, B, 0.4)


def draw_fine_columns(key, part):
    key = jax.random.fold_in(key, 12)
    first_key, second_key = jax.random.split(key)
    own_rows = (jnp.arange(NFB) % NBLK).astype(jnp.int32)
    halo_rows = NBLK + jnp.arange(4, dtype=jnp.int32)[None, :] * HS + jax.random.randint(first_key, (NFB, 4), 0, HS)
    local_rows = jax.random.randint(second_key, (NFB, K - 5), 0, NBLK)
    return jnp.concatenate([own_rows[:, None], halo_rows.astype(jnp.int32), local_rows.astype(jnp.int32)], axis=1).astype(jnp.int32)


def draw_send_lists(key, part):
    key = jax.random.fold_in(key, 13)
    first_key, second_key = jax.random.split(key)
    counts = jax.random.randint(first_key, (DEVICES, 4), HS // 2, HS + 1)
    counts = counts.at[0, 0].set(HS)
    entries = jax.random.randint(second_key, (DEVICES, 4, HS), 0, NBLK)
    slots = jnp.arange(HS, dtype=jnp.int32)
    return jnp.where(slots[None, None, :] < counts[:, :, None], entries, -1).astype(jnp.int32)


def draw_smoother(key, part):
    key = jax.random.fold_in(key, 14)
    return near_inverse(key, NFB, B, 0.15).astype(jnp.bfloat16)


def draw_agg_map(key, part):
    key = jax.random.fold_in(key, 15)
    drawn = jax.random.randint(key, (NFB,), 0, NAGG)
    local_rows = (jnp.arange(NFB) % NBLK).astype(jnp.int32)
    return jnp.where(local_rows < NAGG, local_rows, drawn).astype(jnp.int32)


def draw_coarse_blocks(key, part):
    key = jax.random.fold_in(key, 16)
    return dominant_blocks(key, NCOARSE, KC, BC, 0.4)


def draw_coarse_columns(key, part):
    key = jax.random.fold_in(key, 17)
    near_key, far_key = jax.random.split(key)
    own_rows = jnp.arange(NCOARSE, dtype=jnp.int32)
    device = own_rows // NAGG
    sec_index = device // N_DOM
    dom_index = device % N_DOM
    dom_steps = jnp.array([-1, 1, 0, 0], dtype=jnp.int32)
    sec_steps = jnp.array([0, 0, -1, 1], dtype=jnp.int32)
    next_dom = dom_index[:, None] + dom_steps[None, :]
    next_sec = sec_index[:, None] + sec_steps[None, :]
    valid = (next_dom >= 0) & (next_dom < N_DOM) & (next_sec >= 0) & (next_sec < N_SEC)
    neighbour = (next_sec * N_DOM + next_dom) * NAGG + jax.random.randint(near_key, (NCOARSE, 4), 0, NAGG).astype(jnp.int32)
    near_rows = jnp.where(valid, neighbour, own_rows[:, None])
    far_rows = jax.random.randint(far_key, (NCOARSE, KC - 5), 0, NCOARSE).astype(jnp.int32)
    return jnp.concatenate([own_rows[:, None], near_rows.astype(jnp.int32), far_rows], axis=1).astype(jnp.int32)


def draw_coarse_smoother(key, part):
    key = jax.random.fold_in(key, 18)
    return near_inverse(key, NCOARSE, BC, 0.25)


def shard_levels(key, shape, shards, least, top_value):
    factor_of, own = 1.0, jax.random.fold_in(key, 6)
    for position, blocks in shards:
        steps = jnp.exp(jax.random.uniform(jax.random.fold_in(own, position), (blocks,), jnp.float32, least / len(shards), top_value / len(shards)))
        factor_of = factor_of * jnp.repeat(steps, shape[position] // blocks).reshape([-1 if axis == position else 1 for axis in range(len(shape))])
    return factor_of


def normal_values(key, shape, scale, reach, cuts=(), held_as=jnp.bfloat16):
    values = scale * jax.random.normal(key, shape, jnp.float32)
    if cuts:
        values = values * shard_levels(key, shape, cuts, -0.22, 0.18)
    return jnp.clip(values, -reach, reach).astype(held_as)


def setup_inputs(seed: int = 0) -> dict:
    streams_of = jax.random.split(jax.random.key(seed), 11)
    rhs = normal_values(streams_of[0], (NFB, B * R), 1.0, 6.0, ((0, 32),), jnp.float32)
    fine_blocks = draw_fine_blocks(jax.random.fold_in(streams_of[10], 71), 0)
    fine_columns = draw_fine_columns(jax.random.fold_in(streams_of[10], 71), 0)
    send_lists = draw_send_lists(jax.random.fold_in(streams_of[10], 71), 0)
    smoother = draw_smoother(jax.random.fold_in(streams_of[10], 71), 0)
    prolong = normal_values(streams_of[5], (NFB, B * BC), 0.7, 4.1875, ((0, 32),))
    agg_map = draw_agg_map(jax.random.fold_in(streams_of[10], 71), 0)
    coarse_blocks = draw_coarse_blocks(jax.random.fold_in(streams_of[10], 71), 0)
    coarse_columns = draw_coarse_columns(jax.random.fold_in(streams_of[10], 71), 0)
    coarse_smoother = draw_coarse_smoother(jax.random.fold_in(streams_of[10], 71), 0)
    return dict(rhs=rhs, fine_blocks=fine_blocks, fine_columns=fine_columns, send_lists=send_lists, smoother=smoother, prolong=prolong, agg_map=agg_map, coarse_blocks=coarse_blocks, coarse_columns=coarse_columns, coarse_smoother=coarse_smoother)


def fine_apply(vector, matrix_tiles, columns, lists):
    chosen = jnp.clip(lists, 0, NBLK - 1).reshape(DEVICES, 4 * HS).astype(jnp.int32)

    def select_rows(block_rows, index):
        return block_rows[index]

    sent = jax.vmap(select_rows)(vector, chosen)
    present = (lists >= 0).reshape(DEVICES, 4 * HS)[..., None]
    sent = jnp.where(present, sent, jnp.zeros((), vector.dtype))
    grid = sent.reshape(N_SEC, N_DOM, 4, HS, B * R)
    zero_dom = jnp.zeros((N_SEC, 1, HS, B * R), vector.dtype)
    zero_sec = jnp.zeros((1, N_DOM, HS, B * R), vector.dtype)
    lower_dom = jnp.concatenate([zero_dom, grid[:, :-1, 0]], axis=1)
    upper_dom = jnp.concatenate([grid[:, 1:, 1], zero_dom], axis=1)
    lower_sec = jnp.concatenate([zero_sec, grid[:-1, :, 2]], axis=0)
    upper_sec = jnp.concatenate([grid[1:, :, 3], zero_sec], axis=0)
    received = jnp.stack([lower_dom, upper_dom, lower_sec, upper_sec], axis=2).reshape(DEVICES, 4 * HS, B * R)
    extended = jnp.concatenate([vector, received], axis=1)

    def one_device(pieces):
        ext_rows, tiles, cols = pieces
        picked = ext_rows[cols].astype(jnp.float32).reshape(NBLK, K, B, R)
        mats = tiles.astype(jnp.float32).reshape(NBLK, K, B, B)
        return jnp.einsum("nkbc,nkcr->nbr", mats, picked, precision=lax.Precision.HIGHEST).reshape(NBLK, B * R)

    return lax.map(one_device, (extended, matrix_tiles, columns))


def relax_apply(smooth_tiles, vector):
    def one_device(pieces):
        tiles, field = pieces
        mats = tiles.astype(jnp.float32).reshape(NBLK, B, B)
        values = field.astype(jnp.float32).reshape(NBLK, B, R)
        return jnp.einsum("nbc,ncr->nbr", mats, values, precision=lax.Precision.HIGHEST).reshape(NBLK, B * R)

    return lax.map(one_device, (smooth_tiles, vector))


def reference(rhs, fine_blocks, fine_columns, send_lists, smoother, prolong, agg_map, coarse_blocks, coarse_columns, coarse_smoother):
    right = rhs.reshape(DEVICES, NBLK, B * R)
    matrix_tiles = fine_blocks.reshape(DEVICES, NBLK, K, B * B)
    columns = fine_columns.reshape(DEVICES, NBLK, K)
    smooth_tiles = smoother.reshape(DEVICES, NBLK, B * B)

    def sweep(iterate):
        residual = right - fine_apply(iterate, matrix_tiles, columns, send_lists)
        return iterate + relax_apply(smooth_tiles, residual.astype(jnp.bfloat16))

    iterate = relax_apply(smooth_tiles, right.astype(jnp.bfloat16))
    for repeat in range(NPRE - 1):
        iterate = sweep(iterate)
    residual = right - fine_apply(iterate, matrix_tiles, columns, send_lists)
    prolong_tiles = prolong.astype(jnp.float32).reshape(NFB, B, BC)
    residual_tiles = residual.astype(jnp.bfloat16).astype(jnp.float32).reshape(NFB, B, R)
    local_terms = jnp.einsum("nbj,nbr->njr", prolong_tiles, residual_tiles, precision=lax.Precision.HIGHEST).reshape(NFB, BC * R)
    owner = (jnp.arange(NFB) // NBLK).astype(jnp.int32)
    target = (owner * NAGG + agg_map).astype(jnp.int32)
    coarse_rhs = jnp.zeros((NCOARSE, BC * R), jnp.float32).at[target].add(local_terms)
    coarse_mats = coarse_blocks.reshape(NCOARSE, KC, BC, BC)
    inverse = coarse_smoother.reshape(NCOARSE, BC, BC)

    def precond(field):
        return jnp.einsum("nij,njr->nir", inverse, field.reshape(NCOARSE, BC, R), precision=lax.Precision.HIGHEST).reshape(NCOARSE, BC * R)

    coarse_solution = precond(coarse_rhs)
    for repeat in range(CITERS):
        fetched = coarse_solution[coarse_columns].reshape(NCOARSE, KC, BC, R)
        applied = jnp.einsum("nkij,nkjr->nir", coarse_mats, fetched, precision=lax.Precision.HIGHEST).reshape(NCOARSE, BC * R)
        coarse_solution = coarse_solution + precond(coarse_rhs - applied)
    picked = coarse_solution[target].reshape(NFB, BC, R)
    correction = jnp.einsum("nbj,njr->nbr", prolong_tiles, picked, precision=lax.Precision.HIGHEST).reshape(DEVICES, NBLK, B * R)
    iterate = iterate + correction
    for repeat in range(NPOST):
        iterate = sweep(iterate)
    return iterate.reshape(NFB, B * R), coarse_solution
```

```python
import functools

import jax
import jax.numpy as jnp
from jax import lax
from jax.experimental import pallas as pl
from jax.experimental.pallas import tpu as pltpu
from jax.sharding import PartitionSpec as P

B = 64
R = 32
BC = 6
K = 8
KC = 8
NPRE = 5
NPOST = 5
CITERS = 4
NAGG = 2
HALF = 4 * B
TURNS = NPRE + NPOST
MESH = pl.DeviceIdType.MESH
DENSE_LIMIT = 1024


def split2(value):
    high = value.astype(jnp.bfloat16)
    return high, (value - high.astype(jnp.float32)).astype(jnp.bfloat16)


def cycle_kernel(
    n_sec, n_dom,
    rhs, fine, smooth, restrict, prolong, coarse_own, lists_own, columns, agg,
    x_out, w_out,
    a_high, a_low, fields, halo, turned, gathered, slots,
    lists_in, lists_scalar, tiles_in, tiles3, dense, dense_high, dense_low, inverse,
    coarse_in, state,
    halo_send, halo_recv, list_send, list_recv, list_local,
    tile_send, tile_recv, coarse_send, coarse_recv,
):
    count = n_sec * n_dom
    rows = 8 * count
    s, d = lax.axis_index("sec"), lax.axis_index("dom")
    me = s * n_dom + d
    links = (
        ((s, d + 1), d < n_dom - 1, d > 0),
        ((s, d - 1), d > 0, d < n_dom - 1),
        ((s + 1, d), s < n_sec - 1, s > 0),
        ((s - 1, d), s > 0, s < n_sec - 1),
    )
    lane = lax.broadcasted_iota(jnp.int32, (1, 128), 1)
    group = lane // R

    def to_others(action):
        def visit(step, carry):
            other = lax.rem(me + step, count)
            action((other // n_dom, lax.rem(other, n_dom)))
            return carry

        lax.fori_loop(1, count, visit, 0)

    barrier = pltpu.get_barrier_semaphore()
    to_others(lambda where: pl.semaphore_signal(barrier, inc=1, device_id=where, device_id_type=MESH))

    def diagonal(product):
        parts = [product[g * B:(g + 1) * B] for g in range(4)]
        return jnp.where(group == 0, parts[0], jnp.where(group == 1, parts[1], jnp.where(group == 2, parts[2], parts[3])))

    def relax(half, value):
        product = jnp.dot(
            smooth[half * HALF:(half + 1) * HALF, :], value.astype(jnp.bfloat16), preferred_element_type=jnp.float32
        )
        return diagonal(product)

    def halo_copy(turn, q):
        return pltpu.make_async_remote_copy(
            src_ref=fields.at[turn], dst_ref=halo.at[turn, q],
            send_sem=halo_send.at[turn, q], recv_sem=halo_recv.at[turn, q],
            device_id=links[q][0], device_id_type=MESH,
        )

    def list_copy(q):
        return pltpu.make_async_remote_copy(
            src_ref=lists_own, dst_ref=lists_in.at[q],
            send_sem=list_send.at[q], recv_sem=list_recv.at[q],
            device_id=links[q][0], device_id_type=MESH,
        )

    def turn_tiles(value, source):
        for half in range(2):
            part = value[half * B:(half + 1) * B, :]
            for step in range(4):
                turned[(source * 2 + half) * 4 + step] = part if step == 0 else pltpu.roll(part, step * R, 1)

    def start_halo(turn):
        for q in range(4):
            @pl.when(links[q][1])
            def _():
                halo_copy(turn, q).start()

    def publish(turn, halves):
        for half in range(2):
            fields[turn, half * B:(half + 1) * B, :] = halves[half]
        start_halo(turn)
        turn_tiles(fields[turn], 0)

    def spread_copy(source, place, send_sem, recv_sem, where):
        return pltpu.make_async_remote_copy(
            src_ref=source, dst_ref=place.at[me], send_sem=send_sem, recv_sem=recv_sem,
            device_id=where, device_id_type=MESH,
        )

    def wait_bytes(place, sem):
        part = place.at[pl.ds(0, count - 1)]
        pltpu.make_async_copy(part, part, sem).wait()

    first = [relax(half, rhs[half * B:(half + 1) * B, :]) for half in range(2)]
    high, low = split2(fine[...])
    a_high[...] = high
    a_low[...] = low
    dense[...] = jnp.zeros_like(dense)
    turned[40:44] = jnp.zeros((4, B, 128), jnp.float32)
    for q in range(4):
        @pl.when(jnp.logical_not(links[q][2]))
        def _():
            lists_in[q] = jnp.full((8, 128), -1, jnp.int32)

    pl.semaphore_wait(barrier, count - 1)
    for q in range(4):
        @pl.when(links[q][1])
        def _():
            list_copy(q).start()
    publish(0, first)
    tiles_in[me] = coarse_own[...]
    to_others(lambda where: spread_copy(coarse_own, tiles_in, tile_send, tile_recv, where).start())
    for q in range(4):
        @pl.when(links[q][2])
        def _():
            list_copy(q).wait_recv()
    to_scalar = pltpu.make_async_copy(lists_in, lists_scalar, list_local)
    to_scalar.start()
    to_scalar.wait()

    def find_slot(index, carry):
        column = columns[index]
        row = index // K
        q = jnp.maximum(column // 8 - 1, 0)
        listed = lists_scalar[q, q, lax.rem(column, 8)]
        place = jnp.where(column < 8, column, jnp.where(listed < 0, 40, (q + 1) * 8 + listed))
        piece = jnp.where(place >= 40, 10, place // 4)
        slots[index] = piece * 4 + lax.rem(row - place + 64, 4)
        return carry

    lax.fori_loop(0, 8 * K, find_slot, 0)

    def residual(turn):
        for q in range(4):
            @pl.when(links[q][2])
            def _():
                halo_copy(turn, q).wait_recv()
                turn_tiles(halo[turn, q], q + 1)
        result = []
        for half in range(2):
            for k in range(K):
                t = [turned[slots[(half * 4 + g) * K + k]] for g in range(4)]
                tile = jnp.where(group == 0, t[0], jnp.where(group == 1, t[1], jnp.where(group == 2, t[2], t[3])))
                high, low = split2(tile)
                gathered[half, k * B:(k + 1) * B, 0:128] = high
                gathered[half, k * B:(k + 1) * B, 128:256] = low
            span = slice(half * HALF, (half + 1) * HALF)
            both = jnp.dot(a_high[span, :], gathered[half], preferred_element_type=jnp.float32)
            rest = jnp.dot(a_low[span, :], gathered[half, :, 0:128], preferred_element_type=jnp.float32)
            product = both[:, 0:128] + both[:, 128:256] + rest
            result.append(rhs[half * B:(half + 1) * B, :] - diagonal(product))
        return result

    def sweep(turn):
        left = residual(turn)
        return [fields[turn, half * B:(half + 1) * B, :] + relax(half, left[half]) for half in range(2)]

    position = lax.broadcasted_iota(jnp.int32, (1, 2 * rows), 1)
    within = lax.rem(position, rows)
    named = jnp.where(lax.rem(position, 8) < BC, (within // 8 * NAGG + position // rows).astype(jnp.float32), -1.0)
    from_lane = lax.rem(lax.broadcasted_iota(jnp.int32, (384, 128), 0), 128)
    to_lane = lax.broadcasted_iota(jnp.int32, (384, 128), 1)

    def pick(wanted):
        chosen = (from_lane == wanted).astype(jnp.float32).astype(jnp.bfloat16)
        return jnp.dot(tiles3[...], chosen, preferred_element_type=jnp.float32)

    def add_blocks(k):
        for a in range(NAGG):
            spread = pick((a * KC + k) * 8 + lax.rem(to_lane, 8))
            names = jnp.broadcast_to(spread.reshape(count, 8, 128)[:, BC:BC + 1, :], (count, 8, 128)).reshape(rows, 128)
            for v in range(2 * rows // 128):
                cut = slice(v * 128, (v + 1) * 128)
                dense[a * rows:(a + 1) * rows, cut] += jnp.where(names == named[:, cut], spread, 0.0)

    def pre_turn(turn, carry):
        publish(turn + 1, sweep(turn))

        @pl.when(turn == 0)
        def _():
            wait_bytes(tiles_in, tile_recv)
            whole = tiles_in[...].reshape(rows, 128)
            high, low = split2(whole)
            tiles3[:, 0:128] = high
            tiles3[:, 128:256] = low
            tiles3[:, 256:384] = (whole - high.astype(jnp.float32) - low.astype(jnp.float32)).astype(jnp.bfloat16)

        add_blocks(2 * turn)
        add_blocks(2 * turn + 1)
        return carry

    lax.fori_loop(0, NPRE - 1, pre_turn, 0)
    for j in range(BC):
        inverse[j] = pick((to_lane // R * KC + j) * 8 + BC)

    left = residual(NPRE - 1)
    sums = [jnp.zeros((8, 128), jnp.float32) for _ in range(NAGG)]
    for half in range(2):
        terms = jnp.dot(
            restrict[half * 32:(half + 1) * 32, :], left[half].astype(jnp.bfloat16), preferred_element_type=jnp.float32
        )
        for g in range(4):
            kept = jnp.where(group == g, terms[g * 8:(g + 1) * 8], 0.0)
            for a in range(NAGG):
                sums[a] = sums[a] + jnp.where(agg[half * 4 + g] == a, kept, 0.0)

    def fold(value):
        value = value + pltpu.roll(value, 64, 1)
        return value + pltpu.roll(value, 32, 1)

    folded = [fold(value) for value in sums]
    coarse_in[me] = jnp.where(group == 0, folded[0], jnp.where(group == 1, folded[1], 0.0))
    to_others(lambda where: spread_copy(coarse_in.at[me], coarse_in, coarse_send, coarse_recv, where).start())
    high, low = split2(dense[...])
    dense_high[...] = high
    dense_low[...] = low
    wait_bytes(coarse_in, coarse_recv)
    right = coarse_in[...].reshape(rows, 128)

    def precond(value):
        tiles = value.reshape(count, 8, 128)
        total = jnp.zeros((rows, 128), jnp.float32)
        for j in range(BC):
            total = total + inverse[j] * jnp.broadcast_to(tiles[:, j:j + 1, :], (count, 8, 128)).reshape(rows, 128)
        return total

    def coarse_turn(step, carry):
        value = state[...]
        value_r, value_l = pltpu.roll(value, R, 1), pltpu.roll(value, 128 - R, 1)
        stacked = jnp.concatenate(
            [jnp.where(group == 0, value, value_r), jnp.where(group == 0, value_l, value)], axis=0
        )
        high, low = split2(stacked)
        both = jnp.dot(dense_high[...], jnp.concatenate([high, low], axis=1), preferred_element_type=jnp.float32)
        rest = jnp.dot(dense_low[...], high, preferred_element_type=jnp.float32)
        product = both[:, 0:128] + both[:, 128:256] + rest
        applied = jnp.where(group == 0, product[0:rows], product[rows:2 * rows])
        inside = lax.rem(lax.broadcasted_iota(jnp.int32, (rows, 1), 0), 8) < BC
        state[...] = value + precond(jnp.where(inside & (group < NAGG), right - applied, 0.0))
        return carry

    state[...] = precond(right)
    lax.fori_loop(0, CITERS, coarse_turn, 0)
    own = state[pl.ds(pl.multiple_of(me * 8, 8), 8), :]
    w_out[...] = own
    answers = [
        fold(jnp.where(group == a, own, 0.0)) for a in range(NAGG)
    ]
    corrected = []
    for half in range(2):
        picked = jnp.zeros((8, 128), jnp.float32)
        for g in range(4):
            for a in range(NAGG):
                picked = picked + jnp.where((group == g) & (agg[half * 4 + g] == a), answers[a], 0.0)
        product = jnp.dot(
            prolong[half * HALF:(half + 1) * HALF, :], picked,
            precision=lax.Precision.HIGHEST, preferred_element_type=jnp.float32,
        )
        corrected.append(fields[NPRE - 1, half * B:(half + 1) * B, :] + diagonal(product))
    publish(NPRE, corrected)

    def post_turn(turn, carry):
        publish(turn + 1, sweep(turn))
        return carry

    lax.fori_loop(NPRE, TURNS - 1, post_turn, 0)
    last = sweep(TURNS - 1)
    for half in range(2):
        x_out[half * B:(half + 1) * B, :] = last[half]

    def drain(turn, carry):
        for q in range(4):
            @pl.when(links[q][1])
            def _():
                halo_copy(turn, q).wait_send()
        return carry

    lax.fori_loop(0, TURNS, drain, 0)
    for q in range(4):
        @pl.when(links[q][1])
        def _():
            list_copy(q).wait_send()
    wait_bytes(tiles_in, tile_send)
    wait_bytes(coarse_in, coarse_send)


def fused_cycle(n_sec, n_dom, rhs, fine_blocks, fine_columns, send_lists, smoother, prolong, agg_map,
                coarse_blocks, coarse_columns, coarse_smoother):
    count = n_sec * n_dom
    rows = 8 * count
    packed = rhs.reshape(2, 4, B, R).transpose(0, 2, 1, 3).reshape(2 * B, 4 * R)
    fine = fine_blocks.reshape(8, K, B, B).transpose(0, 2, 1, 3).reshape(8 * B, K * B)
    smooth = smoother.reshape(8 * B, B)
    tiles = jnp.pad(prolong.reshape(8, B, BC), ((0, 0), (0, 0), (0, 2)))
    restrict = tiles.transpose(0, 2, 1).reshape(64, B)
    lifts = tiles.reshape(8 * B, 8).astype(jnp.float32)
    lists = jnp.pad(send_lists[0], ((0, 4), (0, 120)), constant_values=-1)
    blocks = coarse_blocks.reshape(NAGG, KC, BC, BC)
    inverse = jnp.pad(coarse_smoother.reshape(NAGG, BC, BC).transpose(0, 2, 1), ((0, 0), (0, KC - BC), (0, 0)))
    upper = jnp.concatenate([blocks, inverse[..., None], jnp.zeros_like(inverse)[..., None]], axis=3)
    names = jnp.broadcast_to(coarse_columns.astype(jnp.float32)[:, :, None, None], (NAGG, KC, 1, BC))
    lower = jnp.pad(names, ((0, 0), (0, 0), (0, 1), (0, 2)))
    coarse_own = jnp.concatenate([upper, lower], axis=2).transpose(2, 0, 1, 3).reshape(8, 128)

    vmem = pl.BlockSpec(memory_space=pltpu.VMEM)
    smem = pl.BlockSpec(memory_space=pltpu.SMEM)
    f32, bf16 = jnp.float32, jnp.bfloat16
    x, w = pl.pallas_call(
        functools.partial(cycle_kernel, n_sec, n_dom),
        out_shape=(jax.ShapeDtypeStruct((2 * B, 128), f32), jax.ShapeDtypeStruct((8, 128), f32)),
        in_specs=[vmem] * 7 + [smem] * 2,
        out_specs=(vmem, vmem),
        scratch_shapes=[
            pltpu.VMEM((512, 512), bf16),
            pltpu.VMEM((512, 512), bf16),
            pltpu.VMEM((TURNS, 128, 128), f32),
            pltpu.VMEM((TURNS, 4, 128, 128), f32),
            pltpu.VMEM((44, B, 128), f32),
            pltpu.VMEM((2, 512, 256), bf16),
            pltpu.SMEM((64,), jnp.int32),
            pltpu.VMEM((4, 8, 128), jnp.int32),
            pltpu.SMEM((4, 8, 128), jnp.int32),
            pltpu.VMEM((count, 8, 128), f32),
            pltpu.VMEM((rows, 384), bf16),
            pltpu.VMEM((2 * rows, 2 * rows), f32),
            pltpu.VMEM((2 * rows, 2 * rows), bf16),
            pltpu.VMEM((2 * rows, 2 * rows), bf16),
            pltpu.VMEM((BC, rows, 128), f32),
            pltpu.VMEM((count, 8, 128), f32),
            pltpu.VMEM((rows, 128), f32),
            pltpu.SemaphoreType.DMA((TURNS, 4)),
            pltpu.SemaphoreType.DMA((TURNS, 4)),
            pltpu.SemaphoreType.DMA((4,)),
            pltpu.SemaphoreType.DMA((4,)),
            pltpu.SemaphoreType.DMA,
            pltpu.SemaphoreType.DMA,
            pltpu.SemaphoreType.DMA,
            pltpu.SemaphoreType.DMA,
            pltpu.SemaphoreType.DMA,
        ],
        compiler_params=pltpu.CompilerParams(
            collective_id=0, has_side_effects=True, vmem_limit_bytes=48 * 1024 * 1024
        ),
    )(packed, fine, smooth, restrict, lifts, coarse_own, lists, fine_columns.reshape(64), agg_map)
    solved = x.reshape(2, B, 4, R).transpose(0, 2, 1, 3).reshape(8, B * R)
    coarse = w[:BC, :NAGG * R].reshape(BC, NAGG, R).transpose(1, 0, 2).reshape(NAGG, BC * R)
    return solved, coarse


def passed_along(block, axis, distance):
    devices = range(lax.axis_size(axis))
    route = [(i - distance, i) for i in devices if i - distance in devices]
    return lax.ppermute(block, axis, route)


def coarse_terms(coarse_mats, where_col, piece):
    row_total = coarse_mats.shape[0]
    piece_rows = piece.shape[0]
    inside = (where_col >= 0) & (where_col < piece_rows)
    fetched = jnp.where(inside[..., None], piece[jnp.clip(where_col, 0, piece_rows - 1)], 0.0)
    fetched = fetched.reshape(row_total, KC, BC, R)
    return jnp.einsum(
        "nkij,nkjr->nir", coarse_mats, fetched, precision=lax.Precision.HIGHEST
    ).reshape(row_total, BC * R)


def coarse_solve(coarse_rhs, blocks, smooth_rows, fold_call):
    row_total = coarse_rhs.shape[0]
    coarse_mats = blocks.reshape(row_total, KC, BC, BC)
    inverse = smooth_rows.reshape(row_total, BC, BC)

    def precond(field):
        return jnp.einsum(
            "nij,njr->nir",
            inverse,
            field.reshape(row_total, BC, R),
            precision=lax.Precision.HIGHEST,
        ).reshape(row_total, BC * R)

    answer = precond(coarse_rhs)
    for repeat in range(CITERS):
        applied = fold_call(answer, coarse_mats)
        answer = answer + precond(coarse_rhs - applied)
    return answer


def staged_cycle(
    rhs,
    fine_blocks,
    fine_columns,
    send_lists,
    smoother,
    prolong,
    agg_map,
    coarse_blocks,
    coarse_columns,
    coarse_smoother,
):
    row_count = rhs.shape[0]
    lists = send_lists[0]
    chosen = jnp.clip(lists, 0, row_count - 1)
    present = (lists >= 0)[..., None]
    matrix_tiles = fine_blocks.reshape(row_count, K, B, B)
    smooth_tiles = smoother.reshape(row_count, B, B)
    prolong_tiles = prolong.reshape(row_count, B, BC)

    def apply_fine(vector):
        outgoing = jnp.where(present, vector[chosen], jnp.zeros((), vector.dtype))
        lower_dom = passed_along(outgoing[0], "dom", 1)
        upper_dom = passed_along(outgoing[1], "dom", -1)
        lower_sec = passed_along(outgoing[2], "sec", 1)
        upper_sec = passed_along(outgoing[3], "sec", -1)
        extended = jnp.concatenate([vector, lower_dom, upper_dom, lower_sec, upper_sec], axis=0)
        picked = extended[fine_columns].reshape(row_count, K, B, R)
        return jnp.einsum(
            "nkbc,nkcr->nbr", matrix_tiles, picked, precision=lax.Precision.HIGHEST
        ).reshape(row_count, B * R)

    def relax(vector):
        return jnp.einsum(
            "nbc,ncr->nbr",
            smooth_tiles,
            vector.reshape(row_count, B, R),
            preferred_element_type=jnp.float32,
        ).reshape(row_count, B * R)

    def sweep(iterate):
        residual = rhs - apply_fine(iterate)
        return iterate + relax(residual.astype(jnp.bfloat16))

    iterate = relax(rhs.astype(jnp.bfloat16))
    for repeat in range(NPRE - 1):
        iterate = sweep(iterate)
    residual = rhs - apply_fine(iterate)
    members = agg_map[:, None] == jnp.arange(NAGG, dtype=jnp.int32)[None, :]
    local_terms = jnp.einsum(
        "nbj,nbr->njr",
        prolong_tiles,
        residual.astype(jnp.bfloat16).reshape(row_count, B, R),
        preferred_element_type=jnp.float32,
    ).reshape(row_count, BC * R)
    coarse_rhs = jnp.dot(
        members.astype(jnp.float32).T, local_terms, precision=lax.Precision.HIGHEST
    )
    rhs_all, blocks_all, smooth_all = (
        lax.all_gather(coarse_rhs, "sec", axis=0, tiled=True),
        lax.all_gather(coarse_blocks, "sec", axis=0, tiled=True),
        lax.all_gather(coarse_smoother, "sec", axis=0, tiled=True),
    )
    columns_all = lax.all_gather(coarse_columns, "sec", axis=0, tiled=True)
    spread = lax.axis_size("dom")
    depth = lax.axis_size("sec")
    where_col = (
        columns_all // NAGG % spread * (depth * NAGG)
        + columns_all // (spread * NAGG) * NAGG
        + columns_all % NAGG
    )

    def fold_section(vector, coarse_mats):
        return coarse_terms(
            coarse_mats, where_col, lax.all_gather(vector, "dom", axis=0, tiled=True)
        )

    gathered_answer = coarse_solve(rhs_all, blocks_all, smooth_all, fold_section)
    own_answer = lax.dynamic_slice_in_dim(gathered_answer, lax.axis_index("sec") * NAGG, NAGG, 0)
    selected = jnp.dot(members.astype(jnp.float32), own_answer, precision=lax.Precision.HIGHEST)
    correction = jnp.einsum(
        "nbj,njr->nbr",
        prolong_tiles.astype(jnp.float32),
        selected.reshape(row_count, BC, R),
        precision=lax.Precision.HIGHEST,
    ).reshape(row_count, B * R)
    iterate = iterate + correction
    for repeat in range(NPOST):
        iterate = sweep(iterate)
    return (iterate, own_answer)


def solution(mesh):
    placed = (
        P(("sec", "dom"), None),
        P(("sec", "dom"), None, None),
        P(("sec", "dom"), None),
        P(("sec", "dom"), None, None),
        P(("sec", "dom"), None),
        P(("sec", "dom"), None),
        P(("sec", "dom")),
        P(("sec", "dom"), None, None),
        P(("sec", "dom"), None),
        P(("sec", "dom"), None),
    )
    n_sec, n_dom = mesh.shape["sec"], mesh.shape["dom"]
    fits = 2 * 8 * n_sec * n_dom <= DENSE_LIMIT
    local = functools.partial(fused_cycle, n_sec, n_dom) if fits else staged_cycle
    return jax.shard_map(
        local,
        mesh=mesh,
        in_specs=placed,
        out_specs=(P(("sec", "dom"), None), P(("sec", "dom"), None)),
        check_vma=False,
    )
```

```python
import functools

import jax
import jax.numpy as jnp
from jax import lax
from jax.experimental import pallas as pl
from jax.experimental.pallas import tpu as pltpu
from jax.sharding import PartitionSpec as P

B = 64
R = 32
BC = 6
K = 8
KC = 8
NPRE = 5
NPOST = 5
CITERS = 4
NAGG = 2
HALF = 4 * B
TURNS = NPRE + NPOST
MESH = pl.DeviceIdType.MESH
DENSE_LIMIT = 1024


def split2(value):
    high = value.astype(jnp.bfloat16)
    return high, (value - high.astype(jnp.float32)).astype(jnp.bfloat16)


def cycle_kernel(
    n_sec, n_dom,
    rhs, fine, smooth, restrict, prolong, coarse_own, lists_own, columns, agg,
    x_out, w_out,
    a_plain, a_high, a_low, fields, halo, turned, gathered, slots,
    lists_in, lists_scalar, tiles_in, tiles3, dense, dense_high, dense_low, inverse_high, inverse_low,
    coarse_in, front, total,
    halo_send, halo_recv, list_send, list_recv, list_local,
    tile_send, tile_recv, coarse_send, coarse_recv,
):
    count = n_sec * n_dom
    rows = 8 * count
    s, d = lax.axis_index("sec"), lax.axis_index("dom")
    me = s * n_dom + d
    links = (
        ((s, d + 1), d < n_dom - 1, d > 0),
        ((s, d - 1), d > 0, d < n_dom - 1),
        ((s + 1, d), s < n_sec - 1, s > 0),
        ((s - 1, d), s > 0, s < n_sec - 1),
    )
    lane = lax.broadcasted_iota(jnp.int32, (1, 128), 1)
    group = lane // R

    def to_others(action):
        def visit(step, carry):
            other = lax.rem(me + step, count)
            action((other // n_dom, lax.rem(other, n_dom)))
            return carry

        lax.fori_loop(1, count, visit, 0)

    barrier = pltpu.get_barrier_semaphore()
    to_others(lambda where: pl.semaphore_signal(barrier, inc=1, device_id=where, device_id_type=MESH))

    def diagonal(product):
        parts = [product[g * B:(g + 1) * B] for g in range(4)]
        return jnp.where(group == 0, parts[0], jnp.where(group == 1, parts[1], jnp.where(group == 2, parts[2], parts[3])))

    def relax(half, value):
        product = jnp.dot(
            smooth[half * HALF:(half + 1) * HALF, :], value.astype(jnp.bfloat16), preferred_element_type=jnp.float32
        )
        return diagonal(product)

    def halo_copy(turn, q):
        return pltpu.make_async_remote_copy(
            src_ref=fields.at[turn], dst_ref=halo.at[turn, q],
            send_sem=halo_send.at[turn, q], recv_sem=halo_recv.at[turn, q],
            device_id=links[q][0], device_id_type=MESH,
        )

    def list_copy(q):
        return pltpu.make_async_remote_copy(
            src_ref=lists_own, dst_ref=lists_in.at[q],
            send_sem=list_send.at[q], recv_sem=list_recv.at[q],
            device_id=links[q][0], device_id_type=MESH,
        )

    def turn_tiles(value, source):
        for half in range(2):
            part = value[half * B:(half + 1) * B, :]
            for step in range(4):
                turned[(source * 2 + half) * 4 + step] = part if step == 0 else pltpu.roll(part, step * R, 1)

    def start_halo(turn):
        for q in range(4):
            @pl.when(links[q][1])
            def _():
                halo_copy(turn, q).start()

    def publish(turn, halves):
        for half in range(2):
            fields[turn, half * B:(half + 1) * B, :] = halves[half]
        start_halo(turn)
        turn_tiles(fields[turn], 0)

    def spread_copy(source, place, send_sem, recv_sem, where):
        return pltpu.make_async_remote_copy(
            src_ref=source, dst_ref=place.at[me], send_sem=send_sem, recv_sem=recv_sem,
            device_id=where, device_id_type=MESH,
        )

    def wait_bytes(place, sem):
        part = place.at[pl.ds(0, count - 1)]
        pltpu.make_async_copy(part, part, sem).wait()

    first = [relax(half, rhs[half * B:(half + 1) * B, :]) for half in range(2)]
    dense[...] = jnp.zeros_like(dense)
    turned[40:44] = jnp.zeros((4, B, 128), jnp.float32)
    for q in range(4):
        @pl.when(jnp.logical_not(links[q][2]))
        def _():
            lists_in[q] = jnp.full((8, 128), -1, jnp.int32)

    pl.semaphore_wait(barrier, count - 1)
    for q in range(4):
        @pl.when(links[q][1])
        def _():
            list_copy(q).start()
    publish(0, first)
    tiles_in[me] = coarse_own[...]
    to_others(lambda where: spread_copy(coarse_own, tiles_in, tile_send, tile_recv, where).start())
    for n in range(8):
        split_rows = fine[n].reshape(K, B // 2, 128)
        for pair in range(K // 2):
            one, two = split_rows[2 * pair], split_rows[2 * pair + 1]
            even = jnp.where(lane < B, one, pltpu.roll(two, B, 1))
            odd = jnp.where(lane < B, pltpu.roll(one, B, 1), two)
            a_plain[pair, pl.ds(n * B, B // 2, stride=2), :] = even
            a_plain[pair, pl.ds(n * B + 1, B // 2, stride=2), :] = odd
    for pair in range(K // 2):
        high, low = split2(a_plain[pair])
        a_high[:, pair * 128:(pair + 1) * 128] = high
        a_low[:, pair * 128:(pair + 1) * 128] = low
    for q in range(4):
        @pl.when(links[q][2])
        def _():
            list_copy(q).wait_recv()
    to_scalar = pltpu.make_async_copy(lists_in, lists_scalar, list_local)
    to_scalar.start()
    to_scalar.wait()

    def find_slot(index, carry):
        column = columns[index]
        row = index // K
        q = jnp.maximum(column // 8 - 1, 0)
        listed = lists_scalar[q, q, lax.rem(column, 8)]
        place = jnp.where(column < 8, column, jnp.where(listed < 0, 40, (q + 1) * 8 + listed))
        piece = jnp.where(place >= 40, 10, place // 4)
        slots[index] = piece * 4 + lax.rem(row - place + 64, 4)
        return carry

    lax.fori_loop(0, 8 * K, find_slot, 0)

    def residual(turn, exact):
        for q in range(4):
            @pl.when(links[q][2])
            def _():
                halo_copy(turn, q).wait_recv()
                turn_tiles(halo[turn, q], q + 1)
        result = []
        for half in range(2):
            for k in range(K):
                t = [turned[slots[(half * 4 + g) * K + k]] for g in range(4)]
                tile = jnp.where(group == 0, t[0], jnp.where(group == 1, t[1], jnp.where(group == 2, t[2], t[3])))
                high, low = split2(tile)
                gathered[half, k * B:(k + 1) * B, 0:128] = high
                gathered[half, k * B:(k + 1) * B, 128:256] = low
            span = slice(half * HALF, (half + 1) * HALF)
            both = jnp.dot(a_high[span, :], gathered[half], preferred_element_type=jnp.float32)
            product = both[:, 0:128] + both[:, 128:256]
            if exact:
                product += jnp.dot(a_low[span, :], gathered[half, :, 0:128], preferred_element_type=jnp.float32)
            result.append(rhs[half * B:(half + 1) * B, :] - diagonal(product))
        return result

    def sweep(turn, exact):
        left = residual(turn, exact)
        return [fields[turn, half * B:(half + 1) * B, :] + relax(half, left[half]) for half in range(2)]

    position = lax.broadcasted_iota(jnp.int32, (1, 2 * rows), 1)
    within = lax.rem(position, rows)
    named = jnp.where(lax.rem(position, 8) < BC, (within // 8 * NAGG + position // rows).astype(jnp.float32), -1.0)
    from_lane = lax.rem(lax.broadcasted_iota(jnp.int32, (384, 128), 0), 128)
    to_lane = lax.broadcasted_iota(jnp.int32, (384, 128), 1)

    def pick(wanted):
        chosen = (from_lane == wanted).astype(jnp.float32).astype(jnp.bfloat16)
        return jnp.dot(tiles3[...], chosen, preferred_element_type=jnp.float32)

    def add_blocks(k):
        for a in range(NAGG):
            spread = pick((a * KC + k) * 8 + lax.rem(to_lane, 8))
            names = jnp.broadcast_to(spread.reshape(count, 8, 128)[:, BC:BC + 1, :], (count, 8, 128)).reshape(rows, 128)
            for v in range(2 * rows // 128):
                cut = slice(v * 128, (v + 1) * 128)
                dense[a * rows:(a + 1) * rows, cut] += jnp.where(names == named[:, cut], spread, 0.0)

    def three_terms(high, low, right_high, right_low):
        both = jnp.dot(jnp.concatenate([high, low], axis=0), right_high, preferred_element_type=jnp.float32)
        rest = jnp.dot(high, right_low, preferred_element_type=jnp.float32)
        return both[0:16] + both[16:32] + rest

    def smoothed_front():
        high, low = split2(front[...])
        parts = []
        for a in range(NAGG):
            cut = slice(a * rows, (a + 1) * rows)
            parts.append(three_terms(high[:, cut], low[:, cut], inverse_high[a], inverse_low[a]))
        return jnp.concatenate(parts, axis=1)

    def grow():
        moved = smoothed_front()
        total[...] += moved
        high, low = split2(moved)
        front[...] -= three_terms(high, low, dense_high[...], dense_low[...])

    def pre_turn(turn, carry):
        publish(turn + 1, sweep(turn, True))

        @pl.when(turn == 0)
        def _():
            wait_bytes(tiles_in, tile_recv)
            whole = tiles_in[...].reshape(rows, 128)
            high, low = split2(whole)
            tiles3[:, 0:128] = high
            tiles3[:, 128:256] = low
            tiles3[:, 256:384] = (whole - high.astype(jnp.float32) - low.astype(jnp.float32)).astype(jnp.bfloat16)

        @pl.when(turn < 2)
        def _():
            for i in range(3):
                add_blocks(3 * turn + i)

        @pl.when(turn == 2)
        def _():
            add_blocks(6)
            add_blocks(7)
            row_part = lax.broadcasted_iota(jnp.int32, (rows, 1), 0) // 8
            for a in range(NAGG):
                spread = pick((a * KC + lax.rem(to_lane, 8)) * 8 + BC)
                for v in range(rows // 128):
                    column_part = (lane + v * 128) // 8
                    high, low = split2(jnp.where(row_part == column_part, spread, 0.0))
                    inverse_high[a, :, v * 128:(v + 1) * 128] = high
                    inverse_low[a, :, v * 128:(v + 1) * 128] = low
            high, low = split2(dense[...])
            dense_high[...] = high
            dense_low[...] = low
            index = lax.broadcasted_iota(jnp.int32, (2 * 8, 1), 0)
            wanted = index // 8 * rows + me * 8 + lax.rem(index, 8)
            front[...] = jnp.where((wanted == position) & (lax.rem(index, 8) < BC), 1.0, 0.0)
            total[...] = jnp.zeros_like(total)

        @pl.when(turn == 3)
        def _():
            grow()
            grow()

        return carry

    lax.fori_loop(0, NPRE - 1, pre_turn, 0)

    left = residual(NPRE - 1, True)
    sums = [jnp.zeros((8, 128), jnp.float32) for _ in range(NAGG)]
    for half in range(2):
        terms = jnp.dot(
            restrict[half * 32:(half + 1) * 32, :], left[half].astype(jnp.bfloat16), preferred_element_type=jnp.float32
        )
        for g in range(4):
            kept = jnp.where(group == g, terms[g * 8:(g + 1) * 8], 0.0)
            for a in range(NAGG):
                sums[a] = sums[a] + jnp.where(agg[half * 4 + g] == a, kept, 0.0)

    def fold(value):
        value = value + pltpu.roll(value, 64, 1)
        return value + pltpu.roll(value, 32, 1)

    folded = [fold(value) for value in sums]
    coarse_in[me] = jnp.where(group == 0, folded[0], jnp.where(group == 1, folded[1], 0.0))
    to_others(lambda where: spread_copy(coarse_in.at[me], coarse_in, coarse_send, coarse_recv, where).start())
    for _ in range(CITERS - 2):
        grow()
    solve = total[...] + smoothed_front()
    solve_high, solve_low = split2(solve)
    wait_bytes(coarse_in, coarse_recv)
    right_high, right_low = split2(coarse_in[...].reshape(rows, 128))
    pieces = [
        three_terms(
            solve_high[:, a * rows:(a + 1) * rows], solve_low[:, a * rows:(a + 1) * rows], right_high, right_low
        )
        for a in range(NAGG)
    ]
    own = jnp.where(group == 0, pieces[0] + pltpu.roll(pieces[1], 128 - R, 1), 0.0)
    answers = [fold(own[a * 8:(a + 1) * 8]) for a in range(NAGG)]
    w_out[...] = jnp.where(group == 0, answers[0], answers[1])
    corrected = []
    for half in range(2):
        picked = jnp.zeros((8, 128), jnp.float32)
        for g in range(4):
            for a in range(NAGG):
                picked = picked + jnp.where((group == g) & (agg[half * 4 + g] == a), answers[a], 0.0)
        product = jnp.dot(
            prolong[half * HALF:(half + 1) * HALF, :], picked,
            precision=lax.Precision.HIGHEST, preferred_element_type=jnp.float32,
        )
        corrected.append(fields[NPRE - 1, half * B:(half + 1) * B, :] + diagonal(product))
    publish(NPRE, corrected)

    def post_turn(turn, carry):
        publish(turn + 1, sweep(turn, False))
        return carry

    lax.fori_loop(NPRE, TURNS - 1, post_turn, 0)
    last = sweep(TURNS - 1, False)
    for half in range(2):
        x_out[half * B:(half + 1) * B, :] = last[half]

    def drain(turn, carry):
        for q in range(4):
            @pl.when(links[q][1])
            def _():
                halo_copy(turn, q).wait_send()
        return carry

    lax.fori_loop(0, TURNS, drain, 0)
    for q in range(4):
        @pl.when(links[q][1])
        def _():
            list_copy(q).wait_send()
    wait_bytes(tiles_in, tile_send)
    wait_bytes(coarse_in, coarse_send)


def fused_cycle(n_sec, n_dom, rhs, fine_blocks, fine_columns, send_lists, smoother, prolong, agg_map,
                coarse_blocks, coarse_columns, coarse_smoother):
    count = n_sec * n_dom
    rows = 8 * count
    packed = rhs.reshape(2, 4, B, R).transpose(0, 2, 1, 3).reshape(2 * B, 4 * R)
    smooth = smoother.reshape(8 * B, B)
    tiles = jnp.pad(prolong.reshape(8, B, BC), ((0, 0), (0, 0), (0, 2)))
    restrict = tiles.transpose(0, 2, 1).reshape(64, B)
    lifts = tiles.reshape(8 * B, 8).astype(jnp.float32)
    lists = jnp.pad(send_lists[0], ((0, 4), (0, 120)), constant_values=-1)
    blocks = coarse_blocks.reshape(NAGG, KC, BC, BC)
    inverse = jnp.pad(coarse_smoother.reshape(NAGG, BC, BC).transpose(0, 2, 1), ((0, 0), (0, KC - BC), (0, 0)))
    upper = jnp.concatenate([blocks, inverse[..., None], jnp.zeros_like(inverse)[..., None]], axis=3)
    names = jnp.broadcast_to(coarse_columns.astype(jnp.float32)[:, :, None, None], (NAGG, KC, 1, BC))
    lower = jnp.pad(names, ((0, 0), (0, 0), (0, 1), (0, 2)))
    coarse_own = jnp.concatenate([upper, lower], axis=2).transpose(2, 0, 1, 3).reshape(8, 128)

    vmem = pl.BlockSpec(memory_space=pltpu.VMEM)
    smem = pl.BlockSpec(memory_space=pltpu.SMEM)
    f32, bf16 = jnp.float32, jnp.bfloat16
    x, w = pl.pallas_call(
        functools.partial(cycle_kernel, n_sec, n_dom),
        out_shape=(jax.ShapeDtypeStruct((2 * B, 128), f32), jax.ShapeDtypeStruct((8, 128), f32)),
        in_specs=[vmem] * 7 + [smem] * 2,
        out_specs=(vmem, vmem),
        scratch_shapes=[
            pltpu.VMEM((4, 512, 128), f32),
            pltpu.VMEM((512, 512), bf16),
            pltpu.VMEM((512, 512), bf16),
            pltpu.VMEM((TURNS, 128, 128), f32),
            pltpu.VMEM((TURNS, 4, 128, 128), f32),
            pltpu.VMEM((44, B, 128), f32),
            pltpu.VMEM((2, 512, 256), bf16),
            pltpu.SMEM((64,), jnp.int32),
            pltpu.VMEM((4, 8, 128), jnp.int32),
            pltpu.SMEM((4, 8, 128), jnp.int32),
            pltpu.VMEM((count, 8, 128), f32),
            pltpu.VMEM((rows, 384), bf16),
            pltpu.VMEM((2 * rows, 2 * rows), f32),
            pltpu.VMEM((2 * rows, 2 * rows), bf16),
            pltpu.VMEM((2 * rows, 2 * rows), bf16),
            pltpu.VMEM((NAGG, rows, rows), bf16),
            pltpu.VMEM((NAGG, rows, rows), bf16),
            pltpu.VMEM((count, 8, 128), f32),
            pltpu.VMEM((16, 2 * rows), f32),
            pltpu.VMEM((16, 2 * rows), f32),
            pltpu.SemaphoreType.DMA((TURNS, 4)),
            pltpu.SemaphoreType.DMA((TURNS, 4)),
            pltpu.SemaphoreType.DMA((4,)),
            pltpu.SemaphoreType.DMA((4,)),
            pltpu.SemaphoreType.DMA,
            pltpu.SemaphoreType.DMA,
            pltpu.SemaphoreType.DMA,
            pltpu.SemaphoreType.DMA,
            pltpu.SemaphoreType.DMA,
        ],
        compiler_params=pltpu.CompilerParams(
            collective_id=0, has_side_effects=True, vmem_limit_bytes=48 * 1024 * 1024
        ),
    )(packed, fine_blocks, smooth, restrict, lifts, coarse_own, lists, fine_columns.reshape(64), agg_map)
    solved = x.reshape(2, B, 4, R).transpose(0, 2, 1, 3).reshape(8, B * R)
    coarse = w[:BC, :NAGG * R].reshape(BC, NAGG, R).transpose(1, 0, 2).reshape(NAGG, BC * R)
    return solved, coarse


def passed_along(block, axis, distance):
    devices = range(lax.axis_size(axis))
    route = [(i - distance, i) for i in devices if i - distance in devices]
    return lax.ppermute(block, axis, route)


def coarse_terms(coarse_mats, where_col, piece):
    row_total = coarse_mats.shape[0]
    piece_rows = piece.shape[0]
    inside = (where_col >= 0) & (where_col < piece_rows)
    fetched = jnp.where(inside[..., None], piece[jnp.clip(where_col, 0, piece_rows - 1)], 0.0)
    fetched = fetched.reshape(row_total, KC, BC, R)
    return jnp.einsum(
        "nkij,nkjr->nir", coarse_mats, fetched, precision=lax.Precision.HIGHEST
    ).reshape(row_total, BC * R)


def coarse_solve(coarse_rhs, blocks, smooth_rows, fold_call):
    row_total = coarse_rhs.shape[0]
    coarse_mats = blocks.reshape(row_total, KC, BC, BC)
    inverse = smooth_rows.reshape(row_total, BC, BC)

    def precond(field):
        return jnp.einsum(
            "nij,njr->nir",
            inverse,
            field.reshape(row_total, BC, R),
            precision=lax.Precision.HIGHEST,
        ).reshape(row_total, BC * R)

    answer = precond(coarse_rhs)
    for repeat in range(CITERS):
        applied = fold_call(answer, coarse_mats)
        answer = answer + precond(coarse_rhs - applied)
    return answer


def staged_cycle(
    rhs,
    fine_blocks,
    fine_columns,
    send_lists,
    smoother,
    prolong,
    agg_map,
    coarse_blocks,
    coarse_columns,
    coarse_smoother,
):
    row_count = rhs.shape[0]
    lists = send_lists[0]
    chosen = jnp.clip(lists, 0, row_count - 1)
    present = (lists >= 0)[..., None]
    matrix_tiles = fine_blocks.reshape(row_count, K, B, B)
    smooth_tiles = smoother.reshape(row_count, B, B)
    prolong_tiles = prolong.reshape(row_count, B, BC)

    def apply_fine(vector):
        outgoing = jnp.where(present, vector[chosen], jnp.zeros((), vector.dtype))
        lower_dom = passed_along(outgoing[0], "dom", 1)
        upper_dom = passed_along(outgoing[1], "dom", -1)
        lower_sec = passed_along(outgoing[2], "sec", 1)
        upper_sec = passed_along(outgoing[3], "sec", -1)
        extended = jnp.concatenate([vector, lower_dom, upper_dom, lower_sec, upper_sec], axis=0)
        picked = extended[fine_columns].reshape(row_count, K, B, R)
        return jnp.einsum(
            "nkbc,nkcr->nbr", matrix_tiles, picked, precision=lax.Precision.HIGHEST
        ).reshape(row_count, B * R)

    def relax(vector):
        return jnp.einsum(
            "nbc,ncr->nbr",
            smooth_tiles,
            vector.reshape(row_count, B, R),
            preferred_element_type=jnp.float32,
        ).reshape(row_count, B * R)

    def sweep(iterate):
        residual = rhs - apply_fine(iterate)
        return iterate + relax(residual.astype(jnp.bfloat16))

    iterate = relax(rhs.astype(jnp.bfloat16))
    for repeat in range(NPRE - 1):
        iterate = sweep(iterate)
    residual = rhs - apply_fine(iterate)
    members = agg_map[:, None] == jnp.arange(NAGG, dtype=jnp.int32)[None, :]
    local_terms = jnp.einsum(
        "nbj,nbr->njr",
        prolong_tiles,
        residual.astype(jnp.bfloat16).reshape(row_count, B, R),
        preferred_element_type=jnp.float32,
    ).reshape(row_count, BC * R)
    coarse_rhs = jnp.dot(
        members.astype(jnp.float32).T, local_terms, precision=lax.Precision.HIGHEST
    )
    rhs_all, blocks_all, smooth_all = (
        lax.all_gather(coarse_rhs, "sec", axis=0, tiled=True),
        lax.all_gather(coarse_blocks, "sec", axis=0, tiled=True),
        lax.all_gather(coarse_smoother, "sec", axis=0, tiled=True),
    )
    columns_all = lax.all_gather(coarse_columns, "sec", axis=0, tiled=True)
    spread = lax.axis_size("dom")
    depth = lax.axis_size("sec")
    where_col = (
        columns_all // NAGG % spread * (depth * NAGG)
        + columns_all // (spread * NAGG) * NAGG
        + columns_all % NAGG
    )

    def fold_section(vector, coarse_mats):
        return coarse_terms(
            coarse_mats, where_col, lax.all_gather(vector, "dom", axis=0, tiled=True)
        )

    gathered_answer = coarse_solve(rhs_all, blocks_all, smooth_all, fold_section)
    own_answer = lax.dynamic_slice_in_dim(gathered_answer, lax.axis_index("sec") * NAGG, NAGG, 0)
    selected = jnp.dot(members.astype(jnp.float32), own_answer, precision=lax.Precision.HIGHEST)
    correction = jnp.einsum(
        "nbj,njr->nbr",
        prolong_tiles.astype(jnp.float32),
        selected.reshape(row_count, BC, R),
        precision=lax.Precision.HIGHEST,
    ).reshape(row_count, B * R)
    iterate = iterate + correction
    for repeat in range(NPOST):
        iterate = sweep(iterate)
    return (iterate, own_answer)


def solution(mesh):
    placed = (
        P(("sec", "dom"), None),
        P(("sec", "dom"), None, None),
        P(("sec", "dom"), None),
        P(("sec", "dom"), None, None),
        P(("sec", "dom"), None),
        P(("sec", "dom"), None),
        P(("sec", "dom")),
        P(("sec", "dom"), None, None),
        P(("sec", "dom"), None),
        P(("sec", "dom"), None),
    )
    n_sec, n_dom = mesh.shape["sec"], mesh.shape["dom"]
    fits = 2 * 8 * n_sec * n_dom <= DENSE_LIMIT
    local = functools.partial(fused_cycle, n_sec, n_dom) if fits else staged_cycle
    return jax.shard_map(
        local,
        mesh=mesh,
        in_specs=placed,
        out_specs=(P(("sec", "dom"), None), P(("sec", "dom"), None)),
        check_vma=False,
    )
```

```python
import functools

import jax
import jax.numpy as jnp
from jax import lax
from jax.experimental import pallas as pl
from jax.experimental.pallas import tpu as pltpu
from jax.sharding import PartitionSpec as P

B = 64
R = 32
BC = 6
K = 8
KC = 8
NPRE = 5
NPOST = 5
CITERS = 4
NAGG = 2
HALF = 4 * B
TURNS = NPRE + NPOST
MESH = pl.DeviceIdType.MESH
DENSE_LIMIT = 1024


def split2(value):
    high = value.astype(jnp.bfloat16)
    return high, (value - high.astype(jnp.float32)).astype(jnp.bfloat16)


def cycle_kernel(
    n_sec, n_dom,
    rhs, fine, smooth, restrict, prolong, coarse_own, lists_own, columns, agg,
    x_out, w_out,
    a_plain, a_high, a_low, fields, halo, turned, gathered, slots,
    lists_in, lists_scalar, tiles_in, tiles3, dense, dense_high, dense_low, inverse_high, inverse_low,
    coarse_in, front, total,
    halo_send, halo_recv, list_send, list_recv, list_local,
    tile_send, tile_recv, coarse_send, coarse_recv,
):
    count = n_sec * n_dom
    rows = 8 * count
    s, d = lax.axis_index("sec"), lax.axis_index("dom")
    me = s * n_dom + d
    links = (
        ((s, d + 1), d < n_dom - 1, d > 0),
        ((s, d - 1), d > 0, d < n_dom - 1),
        ((s + 1, d), s < n_sec - 1, s > 0),
        ((s - 1, d), s > 0, s < n_sec - 1),
    )
    lane = lax.broadcasted_iota(jnp.int32, (1, 128), 1)
    group = lane // R

    def to_others(action):
        def visit(step, carry):
            other = lax.rem(me + step, count)
            action((other // n_dom, lax.rem(other, n_dom)))
            return carry

        lax.fori_loop(1, count, visit, 0)

    barrier = pltpu.get_barrier_semaphore()
    to_others(lambda where: pl.semaphore_signal(barrier, inc=1, device_id=where, device_id_type=MESH))

    def diagonal(product):
        parts = [product[g * B:(g + 1) * B] for g in range(4)]
        return jnp.where(group == 0, parts[0], jnp.where(group == 1, parts[1], jnp.where(group == 2, parts[2], parts[3])))

    def relax(half, value):
        product = jnp.dot(
            smooth[half * HALF:(half + 1) * HALF, :], value.astype(jnp.bfloat16), preferred_element_type=jnp.float32
        )
        return diagonal(product)

    def halo_copy(turn, q, half):
        return pltpu.make_async_remote_copy(
            src_ref=fields.at[turn, half], dst_ref=halo.at[turn, q, half],
            send_sem=halo_send.at[turn, q, half], recv_sem=halo_recv.at[turn, q, half],
            device_id=links[q][0], device_id_type=MESH,
        )

    def list_copy(q):
        return pltpu.make_async_remote_copy(
            src_ref=lists_own, dst_ref=lists_in.at[q],
            send_sem=list_send.at[q], recv_sem=list_recv.at[q],
            device_id=links[q][0], device_id_type=MESH,
        )

    def turn_tiles(part, source, half):
        for step in range(4):
            turned[(source * 2 + half) * 4 + step] = part if step == 0 else pltpu.roll(part, step * R, 1)

    def publish(turn, make_half):
        for half in range(2):
            fields[turn, half] = make_half(half)
            for q in (2, 3, 0, 1):
                @pl.when(links[q][1])
                def _():
                    halo_copy(turn, q, half).start()
        for half in range(2):
            turn_tiles(fields[turn, half], 0, half)

    def spread_copy(source, place, send_sem, recv_sem, where):
        return pltpu.make_async_remote_copy(
            src_ref=source, dst_ref=place.at[me], send_sem=send_sem, recv_sem=recv_sem,
            device_id=where, device_id_type=MESH,
        )

    def wait_bytes(place, sem):
        part = place.at[pl.ds(0, count - 1)]
        pltpu.make_async_copy(part, part, sem).wait()

    first = [relax(half, rhs[half * B:(half + 1) * B, :]) for half in range(2)]
    dense[...] = jnp.zeros_like(dense)
    turned[40:44] = jnp.zeros((4, B, 128), jnp.float32)
    for q in range(4):
        @pl.when(jnp.logical_not(links[q][2]))
        def _():
            lists_in[q] = jnp.full((8, 128), -1, jnp.int32)

    pl.semaphore_wait(barrier, count - 1)
    for q in range(4):
        @pl.when(links[q][1])
        def _():
            list_copy(q).start()
    publish(0, lambda half: first[half])
    tiles_in[me] = coarse_own[...]
    to_others(lambda where: spread_copy(coarse_own, tiles_in, tile_send, tile_recv, where).start())
    for n in range(8):
        split_rows = fine[n].reshape(K, B // 2, 128)
        for pair in range(K // 2):
            one, two = split_rows[2 * pair], split_rows[2 * pair + 1]
            even = jnp.where(lane < B, one, pltpu.roll(two, B, 1))
            odd = jnp.where(lane < B, pltpu.roll(one, B, 1), two)
            a_plain[pair, pl.ds(n * B, B // 2, stride=2), :] = even
            a_plain[pair, pl.ds(n * B + 1, B // 2, stride=2), :] = odd
    for pair in range(K // 2):
        high, low = split2(a_plain[pair])
        a_high[:, pair * 128:(pair + 1) * 128] = high
        a_low[:, pair * 128:(pair + 1) * 128] = low
    for q in range(4):
        @pl.when(links[q][2])
        def _():
            list_copy(q).wait_recv()
    to_scalar = pltpu.make_async_copy(lists_in, lists_scalar, list_local)
    to_scalar.start()
    to_scalar.wait()

    def find_slot(index, carry):
        column = columns[index]
        row = index // K
        q = jnp.maximum(column // 8 - 1, 0)
        listed = lists_scalar[q, q, lax.rem(column, 8)]
        place = jnp.where(column < 8, column, jnp.where(listed < 0, 40, (q + 1) * 8 + listed))
        piece = jnp.where(place >= 40, 10, place // 4)
        slots[index] = piece * 4 + lax.rem(row - place + 64, 4)
        return carry

    lax.fori_loop(0, 8 * K, find_slot, 0)

    def gather(turn):
        for half in range(2):
            for q in range(4):
                @pl.when(links[q][2])
                def _():
                    halo_copy(turn, q, half).wait_recv()
                    turn_tiles(halo[turn, q, half], q + 1, half)
        for half in range(2):
            for k in range(K):
                t = [turned[slots[(half * 4 + g) * K + k]] for g in range(4)]
                tile = jnp.where(group == 0, t[0], jnp.where(group == 1, t[1], jnp.where(group == 2, t[2], t[3])))
                high, low = split2(tile)
                gathered[half, k * B:(k + 1) * B, 0:128] = high
                gathered[half, k * B:(k + 1) * B, 128:256] = low

    def residual(half, exact):
        span = slice(half * HALF, (half + 1) * HALF)
        both = jnp.dot(a_high[span, :], gathered[half], preferred_element_type=jnp.float32)
        product = both[:, 0:128] + both[:, 128:256]
        if exact:
            product += jnp.dot(a_low[span, :], gathered[half, :, 0:128], preferred_element_type=jnp.float32)
        return rhs[half * B:(half + 1) * B, :] - diagonal(product)

    def sweep(turn, exact):
        gather(turn)
        return lambda half: fields[turn, half] + relax(half, residual(half, exact))

    position = lax.broadcasted_iota(jnp.int32, (1, 2 * rows), 1)
    within = lax.rem(position, rows)
    named = jnp.where(lax.rem(position, 8) < BC, (within // 8 * NAGG + position // rows).astype(jnp.float32), -1.0)
    from_lane = lax.rem(lax.broadcasted_iota(jnp.int32, (384, 128), 0), 128)
    to_lane = lax.broadcasted_iota(jnp.int32, (384, 128), 1)

    def pick(wanted):
        chosen = (from_lane == wanted).astype(jnp.float32).astype(jnp.bfloat16)
        return jnp.dot(tiles3[...], chosen, preferred_element_type=jnp.float32)

    def add_blocks(k):
        for a in range(NAGG):
            spread = pick((a * KC + k) * 8 + lax.rem(to_lane, 8))
            names = jnp.broadcast_to(spread.reshape(count, 8, 128)[:, BC:BC + 1, :], (count, 8, 128)).reshape(rows, 128)
            for v in range(2 * rows // 128):
                cut = slice(v * 128, (v + 1) * 128)
                dense[a * rows:(a + 1) * rows, cut] += jnp.where(names == named[:, cut], spread, 0.0)

    def three_terms(high, low, right_high, right_low):
        both = jnp.dot(jnp.concatenate([high, low], axis=0), right_high, preferred_element_type=jnp.float32)
        rest = jnp.dot(high, right_low, preferred_element_type=jnp.float32)
        return both[0:16] + both[16:32] + rest

    def smoothed_front():
        high, low = split2(front[...])
        parts = []
        for a in range(NAGG):
            cut = slice(a * rows, (a + 1) * rows)
            parts.append(three_terms(high[:, cut], low[:, cut], inverse_high[a], inverse_low[a]))
        return jnp.concatenate(parts, axis=1)

    def grow():
        moved = smoothed_front()
        total[...] += moved
        high, low = split2(moved)
        front[...] -= three_terms(high, low, dense_high[...], dense_low[...])

    def pre_turn(turn, carry):
        publish(turn + 1, sweep(turn, True))

        @pl.when(turn == 0)
        def _():
            wait_bytes(tiles_in, tile_recv)
            whole = tiles_in[...].reshape(rows, 128)
            high, low = split2(whole)
            tiles3[:, 0:128] = high
            tiles3[:, 128:256] = low
            tiles3[:, 256:384] = (whole - high.astype(jnp.float32) - low.astype(jnp.float32)).astype(jnp.bfloat16)

        @pl.when(turn < 2)
        def _():
            for i in range(3):
                add_blocks(3 * turn + i)

        @pl.when(turn == 2)
        def _():
            add_blocks(6)
            add_blocks(7)
            row_part = lax.broadcasted_iota(jnp.int32, (rows, 1), 0) // 8
            for a in range(NAGG):
                spread = pick((a * KC + lax.rem(to_lane, 8)) * 8 + BC)
                for v in range(rows // 128):
                    column_part = (lane + v * 128) // 8
                    high, low = split2(jnp.where(row_part == column_part, spread, 0.0))
                    inverse_high[a, :, v * 128:(v + 1) * 128] = high
                    inverse_low[a, :, v * 128:(v + 1) * 128] = low
            high, low = split2(dense[...])
            dense_high[...] = high
            dense_low[...] = low
            index = lax.broadcasted_iota(jnp.int32, (2 * 8, 1), 0)
            wanted = index // 8 * rows + me * 8 + lax.rem(index, 8)
            front[...] = jnp.where((wanted == position) & (lax.rem(index, 8) < BC), 1.0, 0.0)
            total[...] = jnp.zeros_like(total)

        @pl.when(turn == 3)
        def _():
            grow()
            grow()

        return carry

    lax.fori_loop(0, NPRE - 1, pre_turn, 0)

    gather(NPRE - 1)
    left = [residual(half, True) for half in range(2)]
    sums = [jnp.zeros((8, 128), jnp.float32) for _ in range(NAGG)]
    for half in range(2):
        terms = jnp.dot(
            restrict[half * 32:(half + 1) * 32, :], left[half].astype(jnp.bfloat16), preferred_element_type=jnp.float32
        )
        for g in range(4):
            kept = jnp.where(group == g, terms[g * 8:(g + 1) * 8], 0.0)
            for a in range(NAGG):
                sums[a] = sums[a] + jnp.where(agg[half * 4 + g] == a, kept, 0.0)

    def fold(value):
        value = value + pltpu.roll(value, 64, 1)
        return value + pltpu.roll(value, 32, 1)

    folded = [fold(value) for value in sums]
    coarse_in[me] = jnp.where(group == 0, folded[0], jnp.where(group == 1, folded[1], 0.0))
    to_others(lambda where: spread_copy(coarse_in.at[me], coarse_in, coarse_send, coarse_recv, where).start())
    for _ in range(CITERS - 2):
        grow()
    solve = total[...] + smoothed_front()
    solve_high, solve_low = split2(solve)
    wait_bytes(coarse_in, coarse_recv)
    right_high, right_low = split2(coarse_in[...].reshape(rows, 128))
    pieces = [
        three_terms(
            solve_high[:, a * rows:(a + 1) * rows], solve_low[:, a * rows:(a + 1) * rows], right_high, right_low
        )
        for a in range(NAGG)
    ]
    own = jnp.where(group == 0, pieces[0] + pltpu.roll(pieces[1], 128 - R, 1), 0.0)
    answers = [fold(own[a * 8:(a + 1) * 8]) for a in range(NAGG)]
    w_out[...] = jnp.where(group == 0, answers[0], answers[1])
    corrected = []
    for half in range(2):
        picked = jnp.zeros((8, 128), jnp.float32)
        for g in range(4):
            for a in range(NAGG):
                picked = picked + jnp.where((group == g) & (agg[half * 4 + g] == a), answers[a], 0.0)
        product = jnp.dot(
            prolong[half * HALF:(half + 1) * HALF, :], picked,
            precision=lax.Precision.HIGHEST, preferred_element_type=jnp.float32,
        )
        corrected.append(fields[NPRE - 1, half] + diagonal(product))
    publish(NPRE, lambda half: corrected[half])

    def post_turn(turn, carry):
        publish(turn + 1, sweep(turn, False))
        return carry

    lax.fori_loop(NPRE, TURNS - 1, post_turn, 0)
    last = sweep(TURNS - 1, False)
    for half in range(2):
        x_out[half * B:(half + 1) * B, :] = last(half)

    def drain(turn, carry):
        for q in range(4):
            @pl.when(links[q][1])
            def _():
                for half in range(2):
                    halo_copy(turn, q, half).wait_send()
        return carry

    lax.fori_loop(0, TURNS, drain, 0)
    for q in range(4):
        @pl.when(links[q][1])
        def _():
            list_copy(q).wait_send()
    wait_bytes(tiles_in, tile_send)
    wait_bytes(coarse_in, coarse_send)


def fused_cycle(n_sec, n_dom, rhs, fine_blocks, fine_columns, send_lists, smoother, prolong, agg_map,
                coarse_blocks, coarse_columns, coarse_smoother):
    count = n_sec * n_dom
    rows = 8 * count
    packed = rhs.reshape(2, 4, B, R).transpose(0, 2, 1, 3).reshape(2 * B, 4 * R)
    smooth = smoother.reshape(8 * B, B)
    tiles = jnp.pad(prolong.reshape(8, B, BC), ((0, 0), (0, 0), (0, 2)))
    restrict = tiles.transpose(0, 2, 1).reshape(64, B)
    lifts = tiles.reshape(8 * B, 8).astype(jnp.float32)
    lists = jnp.pad(send_lists[0], ((0, 4), (0, 120)), constant_values=-1)
    blocks = coarse_blocks.reshape(NAGG, KC, BC, BC)
    inverse = jnp.pad(coarse_smoother.reshape(NAGG, BC, BC).transpose(0, 2, 1), ((0, 0), (0, KC - BC), (0, 0)))
    upper = jnp.concatenate([blocks, inverse[..., None], jnp.zeros_like(inverse)[..., None]], axis=3)
    names = jnp.broadcast_to(coarse_columns.astype(jnp.float32)[:, :, None, None], (NAGG, KC, 1, BC))
    lower = jnp.pad(names, ((0, 0), (0, 0), (0, 1), (0, 2)))
    coarse_own = jnp.concatenate([upper, lower], axis=2).transpose(2, 0, 1, 3).reshape(8, 128)

    vmem = pl.BlockSpec(memory_space=pltpu.VMEM)
    smem = pl.BlockSpec(memory_space=pltpu.SMEM)
    f32, bf16 = jnp.float32, jnp.bfloat16
    x, w = pl.pallas_call(
        functools.partial(cycle_kernel, n_sec, n_dom),
        out_shape=(jax.ShapeDtypeStruct((2 * B, 128), f32), jax.ShapeDtypeStruct((8, 128), f32)),
        in_specs=[vmem] * 7 + [smem] * 2,
        out_specs=(vmem, vmem),
        scratch_shapes=[
            pltpu.VMEM((4, 512, 128), f32),
            pltpu.VMEM((512, 512), bf16),
            pltpu.VMEM((512, 512), bf16),
            pltpu.VMEM((TURNS, 2, B, 128), f32),
            pltpu.VMEM((TURNS, 4, 2, B, 128), f32),
            pltpu.VMEM((44, B, 128), f32),
            pltpu.VMEM((2, 512, 256), bf16),
            pltpu.SMEM((64,), jnp.int32),
            pltpu.VMEM((4, 8, 128), jnp.int32),
            pltpu.SMEM((4, 8, 128), jnp.int32),
            pltpu.VMEM((count, 8, 128), f32),
            pltpu.VMEM((rows, 384), bf16),
            pltpu.VMEM((2 * rows, 2 * rows), f32),
            pltpu.VMEM((2 * rows, 2 * rows), bf16),
            pltpu.VMEM((2 * rows, 2 * rows), bf16),
            pltpu.VMEM((NAGG, rows, rows), bf16),
            pltpu.VMEM((NAGG, rows, rows), bf16),
            pltpu.VMEM((count, 8, 128), f32),
            pltpu.VMEM((16, 2 * rows), f32),
            pltpu.VMEM((16, 2 * rows), f32),
            pltpu.SemaphoreType.DMA((TURNS, 4, 2)),
            pltpu.SemaphoreType.DMA((TURNS, 4, 2)),
            pltpu.SemaphoreType.DMA((4,)),
            pltpu.SemaphoreType.DMA((4,)),
            pltpu.SemaphoreType.DMA,
            pltpu.SemaphoreType.DMA,
            pltpu.SemaphoreType.DMA,
            pltpu.SemaphoreType.DMA,
            pltpu.SemaphoreType.DMA,
        ],
        compiler_params=pltpu.CompilerParams(
            collective_id=0, has_side_effects=True, vmem_limit_bytes=48 * 1024 * 1024
        ),
    )(packed, fine_blocks, smooth, restrict, lifts, coarse_own, lists, fine_columns.reshape(64), agg_map)
    solved = x.reshape(2, B, 4, R).transpose(0, 2, 1, 3).reshape(8, B * R)
    coarse = w[:BC, :NAGG * R].reshape(BC, NAGG, R).transpose(1, 0, 2).reshape(NAGG, BC * R)
    return solved, coarse


def passed_along(block, axis, distance):
    devices = range(lax.axis_size(axis))
    route = [(i - distance, i) for i in devices if i - distance in devices]
    return lax.ppermute(block, axis, route)


def coarse_terms(coarse_mats, where_col, piece):
    row_total = coarse_mats.shape[0]
    piece_rows = piece.shape[0]
    inside = (where_col >= 0) & (where_col < piece_rows)
    fetched = jnp.where(inside[..., None], piece[jnp.clip(where_col, 0, piece_rows - 1)], 0.0)
    fetched = fetched.reshape(row_total, KC, BC, R)
    return jnp.einsum(
        "nkij,nkjr->nir", coarse_mats, fetched, precision=lax.Precision.HIGHEST
    ).reshape(row_total, BC * R)


def coarse_solve(coarse_rhs, blocks, smooth_rows, fold_call):
    row_total = coarse_rhs.shape[0]
    coarse_mats = blocks.reshape(row_total, KC, BC, BC)
    inverse = smooth_rows.reshape(row_total, BC, BC)

    def precond(field):
        return jnp.einsum(
            "nij,njr->nir",
            inverse,
            field.reshape(row_total, BC, R),
            precision=lax.Precision.HIGHEST,
        ).reshape(row_total, BC * R)

    answer = precond(coarse_rhs)
    for repeat in range(CITERS):
        applied = fold_call(answer, coarse_mats)
        answer = answer + precond(coarse_rhs - applied)
    return answer


def staged_cycle(
    rhs,
    fine_blocks,
    fine_columns,
    send_lists,
    smoother,
    prolong,
    agg_map,
    coarse_blocks,
    coarse_columns,
    coarse_smoother,
):
    row_count = rhs.shape[0]
    lists = send_lists[0]
    chosen = jnp.clip(lists, 0, row_count - 1)
    present = (lists >= 0)[..., None]
    matrix_tiles = fine_blocks.reshape(row_count, K, B, B)
    smooth_tiles = smoother.reshape(row_count, B, B)
    prolong_tiles = prolong.reshape(row_count, B, BC)

    def apply_fine(vector):
        outgoing = jnp.where(present, vector[chosen], jnp.zeros((), vector.dtype))
        lower_dom = passed_along(outgoing[0], "dom", 1)
        upper_dom = passed_along(outgoing[1], "dom", -1)
        lower_sec = passed_along(outgoing[2], "sec", 1)
        upper_sec = passed_along(outgoing[3], "sec", -1)
        extended = jnp.concatenate([vector, lower_dom, upper_dom, lower_sec, upper_sec], axis=0)
        picked = extended[fine_columns].reshape(row_count, K, B, R)
        return jnp.einsum(
            "nkbc,nkcr->nbr", matrix_tiles, picked, precision=lax.Precision.HIGHEST
        ).reshape(row_count, B * R)

    def relax(vector):
        return jnp.einsum(
            "nbc,ncr->nbr",
            smooth_tiles,
            vector.reshape(row_count, B, R),
            preferred_element_type=jnp.float32,
        ).reshape(row_count, B * R)

    def sweep(iterate):
        residual = rhs - apply_fine(iterate)
        return iterate + relax(residual.astype(jnp.bfloat16))

    iterate = relax(rhs.astype(jnp.bfloat16))
    for repeat in range(NPRE - 1):
        iterate = sweep(iterate)
    residual = rhs - apply_fine(iterate)
    members = agg_map[:, None] == jnp.arange(NAGG, dtype=jnp.int32)[None, :]
    local_terms = jnp.einsum(
        "nbj,nbr->njr",
        prolong_tiles,
        residual.astype(jnp.bfloat16).reshape(row_count, B, R),
        preferred_element_type=jnp.float32,
    ).reshape(row_count, BC * R)
    coarse_rhs = jnp.dot(
        members.astype(jnp.float32).T, local_terms, precision=lax.Precision.HIGHEST
    )
    rhs_all, blocks_all, smooth_all = (
        lax.all_gather(coarse_rhs, "sec", axis=0, tiled=True),
        lax.all_gather(coarse_blocks, "sec", axis=0, tiled=True),
        lax.all_gather(coarse_smoother, "sec", axis=0, tiled=True),
    )
    columns_all = lax.all_gather(coarse_columns, "sec", axis=0, tiled=True)
    spread = lax.axis_size("dom")
    depth = lax.axis_size("sec")
    where_col = (
        columns_all // NAGG % spread * (depth * NAGG)
        + columns_all // (spread * NAGG) * NAGG
        + columns_all % NAGG
    )

    def fold_section(vector, coarse_mats):
        return coarse_terms(
            coarse_mats, where_col, lax.all_gather(vector, "dom", axis=0, tiled=True)
        )

    gathered_answer = coarse_solve(rhs_all, blocks_all, smooth_all, fold_section)
    own_answer = lax.dynamic_slice_in_dim(gathered_answer, lax.axis_index("sec") * NAGG, NAGG, 0)
    selected = jnp.dot(members.astype(jnp.float32), own_answer, precision=lax.Precision.HIGHEST)
    correction = jnp.einsum(
        "nbj,njr->nbr",
        prolong_tiles.astype(jnp.float32),
        selected.reshape(row_count, BC, R),
        precision=lax.Precision.HIGHEST,
    ).reshape(row_count, B * R)
    iterate = iterate + correction
    for repeat in range(NPOST):
        iterate = sweep(iterate)
    return (iterate, own_answer)


def solution(mesh):
    placed = (
        P(("sec", "dom"), None),
        P(("sec", "dom"), None, None),
        P(("sec", "dom"), None),
        P(("sec", "dom"), None, None),
        P(("sec", "dom"), None),
        P(("sec", "dom"), None),
        P(("sec", "dom")),
        P(("sec", "dom"), None, None),
        P(("sec", "dom"), None),
        P(("sec", "dom"), None),
    )
    n_sec, n_dom = mesh.shape["sec"], mesh.shape["dom"]
    fits = 2 * 8 * n_sec * n_dom <= DENSE_LIMIT
    local = functools.partial(fused_cycle, n_sec, n_dom) if fits else staged_cycle
    return jax.shard_map(
        local,
        mesh=mesh,
        in_specs=placed,
        out_specs=(P(("sec", "dom"), None), P(("sec", "dom"), None)),
        check_vma=False,
    )
```
